32 devices in a mesh: blk: 8 (over z, x), win: 4 (over y, core).
Axes of the slice: x: 2, y: 2, z: 4, core: 2. Of those that a mesh axis runs over, the one named last changes fastest.
Arguments:
- traces: bfloat16 [2048, 4, 1024], P('blk', 'win')
- pairs: int32 [8, 2], P('blk'), may hold values from -1 to 15, as said below
Outputs:
- cross: float32 [8, 2, 48, 128, 128], P('blk', None, 'win')
The draws below stay inside these ranges and needn't reach their ends.
Inputs may be any that keep to these rules, and one draw needn't show every extreme that they name: `pairs`: each live pair slot names two blocks held by its owning blk index or by the blk indices just below or just above it. Empty slots hold -1 in both entries.
All inputs are finite; a program needn't handle non-finite values.
Results may differ from the reference program's by a relative error of at most 0.0051.
Values may be sent and summed in bfloat16 or wider, within the bound.
A program may use at most 64 MiB of HBM per device.

```python
import math
import jax
import jax.numpy as jnp
from jax import lax

CH = 128
SAMPLES = 1024
BINS = 48
FIRST_BIN = 8
BLK_DEV = 2
PAIR_DEV = 1
BLOCKS = 16
WINDOWS = 4
ROWS = 2048


def draw_traces(key, part):
    k_chan, k_win, k_base = jax.random.split(key, 3)
    chan_scale = jnp.exp(jax.random.uniform(k_chan, (ROWS, 1, 1), jnp.float32) * math.log(10.0))
    win_scale = jnp.exp(jax.random.uniform(k_win, (1, WINDOWS, 1), jnp.float32) * math.log(10.0))
    base = jax.random.normal(k_base, (ROWS, WINDOWS, SAMPLES), jnp.float32)
    return (base * chan_scale * win_scale * 0.1).astype(jnp.bfloat16)


def draw_pairs(key, part):
    owners = BLOCKS // BLK_DEV
    slots = owners * PAIR_DEV
    k_first, k_second, k_kind, k_drop = jax.random.split(key, 4)
    slot_ids = jnp.arange(slots, dtype=jnp.int32)
    owner = slot_ids // PAIR_DEV
    kind = slot_ids % 4
    extra = jax.random.randint(k_kind, (slots,), 0, 3).astype(jnp.int32)
    kind = jnp.where(kind == 3, extra, kind)
    offset_a = jax.random.randint(k_first, (slots,), 0, BLK_DEV).astype(jnp.int32)
    offset_b = jax.random.randint(k_second, (slots,), 0, BLK_DEV).astype(jnp.int32)
    offset_b = jnp.where(slot_ids % 4 == 0, BLK_DEV - 1, offset_b)
    home = owner * BLK_DEV
    first = jnp.where(kind == 1, home - BLK_DEV + offset_a, home + offset_a)
    second = jnp.where(kind == 2, home + BLK_DEV + offset_b, home + offset_b)
    live = (first >= 0) & (second < BLOCKS)
    dropped = (slot_ids % 4 == 3) & (jax.random.randint(k_drop, (slots,), 0, 4) == 0)
    live = live & jnp.logical_not(dropped)
    first = jnp.where(live, first, -1)
    second = jnp.where(live, second, -1)
    return jnp.stack([first, second], 1).astype(jnp.int32)


def setup_inputs(seed: int = 0) -> dict:
    seeds = jax.random.split(jax.random.key(seed), 3)
    traces = draw_traces(jax.random.fold_in(seeds[2], 71), 0)
    pairs = draw_pairs(jax.random.fold_in(seeds[2], 71), 0)
    return {"traces": traces, "pairs": pairs}


def spectra_table(samples, bins):
    times = jnp.arange(samples, dtype=jnp.int32)[:, None]
    freqs = FIRST_BIN + jnp.arange(bins, dtype=jnp.int32)[None, :]
    phase = (times * freqs % samples).astype(jnp.float32) * (2.0 * math.pi / samples)
    return jnp.stack([jnp.cos(phase), -jnp.sin(phase)], 1).astype(jnp.bfloat16)

def cross_pair(first, second):
    left = jnp.concatenate([first[:, 0], first[:, 1]], 0).astype(jnp.float32)
    turned_left = jnp.concatenate([first[:, 1], first[:, 0]], 0).astype(jnp.float32)
    right = jnp.concatenate([second[:, 0], second[:, 1]], 0).astype(jnp.float32)
    turned_right = jnp.concatenate([second[:, 0], -second[:, 1]], 0).astype(jnp.float32)
    real_part = jnp.einsum('kfi,kfj->fij', left, right)
    imag_part = jnp.einsum('kfi,kfj->fij', turned_left, turned_right)
    return jnp.stack([real_part, imag_part])

def reference(traces, pairs):
    table = spectra_table(SAMPLES, BINS)
    spec = jnp.einsum('rwt,tcf->wcfr', traces.astype(jnp.float32), table.astype(jnp.float32))
    energy = lax.optimization_barrier(jnp.mean(spec * spec, axis=(1, 2)))
    whitened = (spec * lax.rsqrt(energy + 1e-06)[:, None, None, :]).astype(jnp.bfloat16)

    def one_pair(pair):
        start_a = (jnp.maximum(pair[0], 0) * CH).astype(jnp.int32)
        start_b = (jnp.maximum(pair[1], 0) * CH).astype(jnp.int32)
        first = lax.dynamic_slice_in_dim(whitened, start_a, CH, 3)
        second = lax.dynamic_slice_in_dim(whitened, start_b, CH, 3)
        return cross_pair(first, second)
    summed = lax.map(one_pair, pairs)
    live = (pairs[:, 0] >= 0).astype(jnp.float32)
    return summed * (1.0 / math.sqrt(WINDOWS)) * live[:, None, None, None, None]
```

```python
import functools
import math

import jax
import jax.numpy as jnp
import ml_dtypes
import numpy as np
from jax import lax
from jax.experimental import pallas as pl
from jax.experimental.pallas import tpu as pltpu
from jax.sharding import PartitionSpec as P

CH = 128
BINS = 48
FIRST_BIN = 8
MESH = pl.DeviceIdType.MESH


def spectra_rows(samples, wins):
    bins_here = BINS // wins
    depth = -(-2 * bins_here // 8) * 8
    times = np.arange(samples, dtype=np.int32)[None, :]
    freqs = FIRST_BIN + np.arange(BINS, dtype=np.int32)[:, None]
    phase = (times * freqs % samples).astype(np.float32) * np.float32(2.0 * math.pi / samples)
    both = np.stack([np.cos(phase), -np.sin(phase)], 1).astype(ml_dtypes.bfloat16)
    rows = np.zeros((wins, depth, samples), ml_dtypes.bfloat16)
    rows[:, : 2 * bins_here] = both.reshape(wins, 2 * bins_here, samples)
    return rows.reshape(wins * depth, samples)


def exchange(blks, wins, depth, x_ref, table_ref, white, held, send_sem, recv_sem):
    blk = lax.axis_index("blk")
    win = lax.axis_index("win")
    sides = ((-1, blk > 0), (1, blk < blks - 1))

    barrier = pltpu.get_barrier_semaphore()

    def greet(step, first):
        for j in range(first, wins):
            pl.semaphore_signal(
                barrier,
                inc=1,
                device_id=(blk + step, lax.rem(win + j, wins)),
                device_id_type=MESH,
            )

    for step, there in sides:
        pl.when(there)(functools.partial(greet, step, 0))
    greet(0, 1)

    spec = lax.dot_general(
        table_ref[...], x_ref[...], (((1,), (1,)), ((), ())), preferred_element_type=jnp.float32
    )
    energy = jnp.sum(spec * spec, axis=0, keepdims=True) * (1.0 / (2 * BINS))
    whitened = spec * lax.rsqrt(energy + 1e-06)
    for v in range(wins):
        part = whitened[v * depth : (v + 1) * depth]
        white[v] = jnp.concatenate(
            [part[:, b * CH : (b + 1) * CH] for b in range(part.shape[1] // CH)], 0
        ).astype(jnp.bfloat16)

    partners = (wins - 1) + wins * ((blk > 0).astype(jnp.int32) + (blk < blks - 1).astype(jnp.int32))
    pl.semaphore_wait(barrier, partners)

    def copy(step, j):
        v = lax.rem(win + j, wins)
        return pltpu.make_async_remote_copy(
            src_ref=white.at[v],
            dst_ref=held.at[1 - step, win],
            send_sem=send_sem.at[1 + step, j],
            recv_sem=recv_sem.at[1 - step, win],
            device_id=(blk + step, v),
            device_id_type=MESH,
        )

    def arrival(step, j):
        v = lax.rem(win + j, wins)
        return pltpu.make_async_remote_copy(
            src_ref=white.at[v],
            dst_ref=held.at[1 + step, v],
            send_sem=send_sem.at[1 + step, j],
            recv_sem=recv_sem.at[1 + step, v],
            device_id=(blk + step, v),
            device_id_type=MESH,
        )

    def each(make, act):
        def side(step, first):
            for j in range(first, wins):
                getattr(make(step, j), act)()

        for step, there in sides:
            pl.when(there)(functools.partial(side, step, 0))
        side(0, 1)

    each(copy, "start")
    held[1, win] = white[win]
    each(arrival, "wait_recv")
    return lambda: each(copy, "wait_send")


def cross(blks, wins, depth, pairs_ref, held, out_ref):
    blk = lax.axis_index("blk")
    blocks_here = held.shape[2] // depth
    bins_here = BINS // wins
    first, second = pairs_ref[0, 0], pairs_ref[0, 1]
    live = first >= 0

    def block(index):
        place = jnp.where(live, index - (blk - 1) * blocks_here, blocks_here)
        place = jnp.clip(place, 0, 3 * blocks_here - 1)
        rows = held[place // blocks_here].astype(jnp.float32)
        which = place % blocks_here
        chosen = rows[:, :depth]
        for b in range(1, blocks_here):
            chosen = jnp.where(which == b, rows[:, b * depth : (b + 1) * depth], chosen)
        return chosen.reshape(wins * depth, CH)

    a = block(first)
    b = block(second)
    count = wins * depth
    odd = lax.broadcasted_iota(jnp.int32, (count, CH), 0) % 2
    turned = jnp.where(odd == 1, pltpu.roll(b, 1, 0), -pltpu.roll(b, count - 1, 0))
    right = jnp.concatenate([b, turned], 1).astype(jnp.bfloat16)
    left = a.T
    bin_of = (lax.broadcasted_iota(jnp.int32, (CH, count), 1) % depth) // 2
    lefts = jnp.concatenate(
        [jnp.where(bin_of == k, left, 0.0).astype(jnp.bfloat16) for k in range(bins_here)], 0
    )
    both = jnp.dot(lefts, right, preferred_element_type=jnp.float32)
    both = both * jnp.where(live, 1.0 / math.sqrt(wins), 0.0).astype(jnp.float32)
    for k in range(bins_here):
        rows = both[k * CH : (k + 1) * CH]
        out_ref[0, k] = rows[:, :CH]
        out_ref[1, k] = rows[:, CH:]


def kernel(blks, wins, depth, pairs_ref, x_ref, table_ref, out_ref, white, held, send_sem, recv_sem):
    finish = exchange(blks, wins, depth, x_ref, table_ref, white, held, send_sem, recv_sem)
    cross(blks, wins, depth, pairs_ref, held, out_ref)
    finish()


def solution(mesh):
    blks, wins = mesh.shape["blk"], mesh.shape["win"]

    def shards(traces, pairs):
        rows, windows, samples = traces.shape
        assert windows == 1 and pairs.shape[0] == 1
        table = spectra_rows(samples, wins)
        depth = table.shape[0] // wins
        packed = rows // CH * depth
        bins_here = BINS // wins
        out = pl.pallas_call(
            functools.partial(kernel, blks, wins, depth),
            out_shape=jax.ShapeDtypeStruct((2, bins_here, CH, CH), jnp.float32),
            in_specs=[
                pl.BlockSpec(memory_space=pltpu.SMEM),
                pl.BlockSpec(memory_space=pltpu.VMEM),
                pl.BlockSpec(memory_space=pltpu.VMEM),
            ],
            out_specs=pl.BlockSpec(memory_space=pltpu.VMEM),
            scratch_shapes=[
                pltpu.VMEM((wins, packed, CH), jnp.bfloat16),
                pltpu.VMEM((3, wins, packed, CH), jnp.bfloat16),
                pltpu.SemaphoreType.DMA((3, wins)),
                pltpu.SemaphoreType.DMA((3, wins)),
            ],
            compiler_params=pltpu.CompilerParams(
                collective_id=0, has_side_effects=True, vmem_limit_bytes=24 << 20
            ),
        )(pairs, traces.reshape(rows, samples), jnp.asarray(table))
        return out[None]

    return jax.shard_map(
        shards,
        mesh=mesh,
        in_specs=(P("blk", "win", None), P("blk", None)),
        out_specs=P("blk", None, "win", None, None),
        check_vma=False,
    )
```

```python
import functools
import math

import jax
import jax.numpy as jnp
import ml_dtypes
import numpy as np
from jax import lax
from jax.experimental import pallas as pl
from jax.experimental.pallas import tpu as pltpu
from jax.sharding import PartitionSpec as P

CH = 128
BINS = 48
FIRST_BIN = 8
MESH = pl.DeviceIdType.MESH


def spectra_rows(samples, wins):
    bins_here = BINS // wins
    depth = -(-2 * bins_here // 8) * 8
    times = np.arange(samples, dtype=np.int32)[None, :]
    freqs = FIRST_BIN + np.arange(BINS, dtype=np.int32)[:, None]
    phase = (times * freqs % samples).astype(np.float32) * np.float32(2.0 * math.pi / samples)
    both = np.stack([np.cos(phase), -np.sin(phase)], 1).astype(ml_dtypes.bfloat16)
    rows = np.zeros((wins, depth, samples), ml_dtypes.bfloat16)
    rows[:, : 2 * bins_here] = both.reshape(wins, 2 * bins_here, samples)
    return rows.reshape(wins * depth, samples)


def exchange(blks, wins, depth, x_ref, table_ref, white, held, send_sem, recv_sem, loaded):
    blk = lax.axis_index("blk")
    win = lax.axis_index("win")
    sides = ((-1, blk > 0), (1, blk < blks - 1))

    barrier = pltpu.get_barrier_semaphore()

    def greet(step, first):
        for j in range(first, wins):
            pl.semaphore_signal(
                barrier,
                inc=1,
                device_id=(blk + step, lax.rem(win + j, wins)),
                device_id_type=MESH,
            )

    for step, there in sides:
        pl.when(there)(functools.partial(greet, step, 0))
    greet(0, 1)

    loaded()
    spec = lax.dot_general(
        table_ref[...], x_ref[...], (((1,), (1,)), ((), ())), preferred_element_type=jnp.float32
    )
    energy = jnp.sum(spec * spec, axis=0, keepdims=True) * (1.0 / (2 * BINS))
    whitened = spec * lax.rsqrt(energy + 1e-06)
    for v in range(wins):
        part = whitened[v * depth : (v + 1) * depth]
        white[v] = jnp.concatenate(
            [part[:, b * CH : (b + 1) * CH] for b in range(part.shape[1] // CH)], 0
        ).astype(jnp.bfloat16)

    partners = (wins - 1) + wins * ((blk > 0).astype(jnp.int32) + (blk < blks - 1).astype(jnp.int32))
    pl.semaphore_wait(barrier, partners)

    def copy(step, j):
        v = lax.rem(win + j, wins)
        return pltpu.make_async_remote_copy(
            src_ref=white.at[v],
            dst_ref=held.at[1 - step, win],
            send_sem=send_sem.at[1 + step, j],
            recv_sem=recv_sem.at[1 - step, win],
            device_id=(blk + step, v),
            device_id_type=MESH,
        )

    def arrival(step, j):
        v = lax.rem(win + j, wins)
        return pltpu.make_async_remote_copy(
            src_ref=white.at[v],
            dst_ref=held.at[1 + step, v],
            send_sem=send_sem.at[1 + step, j],
            recv_sem=recv_sem.at[1 + step, v],
            device_id=(blk + step, v),
            device_id_type=MESH,
        )

    def each(make, act):
        def side(step, first):
            for j in range(first, wins):
                getattr(make(step, j), act)()

        for step, there in sides:
            pl.when(there)(functools.partial(side, step, 0))
        side(0, 1)

    each(copy, "start")
    held[1, win] = white[win]
    each(arrival, "wait_recv")
    return lambda: each(copy, "wait_send")


def operands(wins, depth, pairs_ref, held, left_ref, right_ref):
    blk = lax.axis_index("blk")
    blocks_here = held.shape[2] // depth
    first, second = pairs_ref[0, 0], pairs_ref[0, 1]
    live = first >= 0

    def block(index):
        place = jnp.where(live, index - (blk - 1) * blocks_here, blocks_here)
        place = jnp.clip(place, 0, 3 * blocks_here - 1)
        rows = held[place // blocks_here].astype(jnp.float32)
        which = place % blocks_here
        chosen = rows[:, :depth]
        for b in range(1, blocks_here):
            chosen = jnp.where(which == b, rows[:, b * depth : (b + 1) * depth], chosen)
        return chosen.reshape(wins * depth, CH)

    count = wins * depth
    left_ref[...] = block(first).T.astype(jnp.bfloat16)
    b = block(second) * jnp.where(live, 1.0 / math.sqrt(wins), 0.0).astype(jnp.float32)
    odd = lax.broadcasted_iota(jnp.int32, (count, CH), 0) % 2
    turned = jnp.where(odd == 1, pltpu.roll(b, 1, 0), -pltpu.roll(b, count - 1, 0))
    right_ref[...] = jnp.concatenate([b, turned], 1).astype(jnp.bfloat16)


def spectra_kernel(
    blks, wins, depth, pairs_ref, x_ref, table_ref, left_ref, right_ref,
    x, table, pairs, white, held, send_sem, recv_sem, load_sem,
):
    loads = [
        pltpu.make_async_copy(src, dst, load_sem.at[i])
        for i, (src, dst) in enumerate(((x_ref, x), (table_ref, table), (pairs_ref, pairs)))
    ]
    for load in loads:
        load.start()

    def loaded():
        for load in loads:
            load.wait()

    finish = exchange(blks, wins, depth, x, table, white, held, send_sem, recv_sem, loaded)
    operands(wins, depth, pairs, held, left_ref, right_ref)
    finish()


def cross_kernel(depth, left_ref, right_ref, out_ref, result, sem):
    bins_here = result.shape[1]
    left, right = left_ref[...], right_ref[...]
    bin_of = (lax.broadcasted_iota(jnp.int32, left.shape, 1) % depth) // 2
    writes = []
    for k in range(bins_here):
        both = jnp.dot(
            jnp.where(bin_of == k, left, jnp.zeros_like(left)), right, preferred_element_type=jnp.float32
        )
        for c in range(2):
            result[c, k] = both[:, c * CH : (c + 1) * CH]
            write = pltpu.make_async_copy(result.at[c, k], out_ref.at[c, k], sem.at[c, k])
            write.start()
            writes.append(write)
    for write in writes:
        write.wait()


def solution(mesh):
    blks, wins = mesh.shape["blk"], mesh.shape["win"]

    def shards(traces, pairs):
        rows, windows, samples = traces.shape
        assert windows == 1 and pairs.shape[0] == 1
        table = spectra_rows(samples, wins)
        count = table.shape[0]
        depth = count // wins
        packed = rows // CH * depth
        bins_here = BINS // wins
        inputs = pairs, traces.reshape(rows, samples), jnp.asarray(table)
        left, right = pl.pallas_call(
            functools.partial(spectra_kernel, blks, wins, depth),
            out_shape=[
                pltpu.VMEM((CH, count), jnp.bfloat16),
                pltpu.VMEM((count, 2 * CH), jnp.bfloat16),
            ],
            in_specs=[pl.BlockSpec(memory_space=pltpu.HBM)] * 3,
            out_specs=[pl.BlockSpec(memory_space=pltpu.VMEM)] * 2,
            scratch_shapes=[
                pltpu.VMEM((rows, samples), jnp.bfloat16),
                pltpu.VMEM((count, samples), jnp.bfloat16),
                pltpu.SMEM((1, 2), jnp.int32),
                pltpu.VMEM((wins, packed, CH), jnp.bfloat16),
                pltpu.VMEM((3, wins, packed, CH), jnp.bfloat16),
                pltpu.SemaphoreType.DMA((3, wins)),
                pltpu.SemaphoreType.DMA((3, wins)),
                pltpu.SemaphoreType.DMA((3,)),
            ],
            compiler_params=pltpu.CompilerParams(
                collective_id=0, has_side_effects=True, vmem_limit_bytes=24 << 20
            ),
        )(*(pltpu.with_memory_space_constraint(a, pltpu.HBM) for a in inputs))
        out = pl.pallas_call(
            functools.partial(cross_kernel, depth),
            out_shape=jax.ShapeDtypeStruct((2, bins_here, CH, CH), jnp.float32),
            in_specs=[pl.BlockSpec(memory_space=pltpu.VMEM)] * 2,
            out_specs=pl.BlockSpec(memory_space=pltpu.HBM),
            scratch_shapes=[
                pltpu.VMEM((2, bins_here, CH, CH), jnp.float32),
                pltpu.SemaphoreType.DMA((2, bins_here)),
            ],
            compiler_params=pltpu.CompilerParams(vmem_limit_bytes=24 << 20),
        )(left, right)
        return out[None]

    return jax.shard_map(
        shards,
        mesh=mesh,
        in_specs=(P("blk", "win", None), P("blk", None)),
        out_specs=P("blk", None, "win", None, None),
        check_vma=False,
    )
```

```python
import functools
import math

import jax
import jax.numpy as jnp
import ml_dtypes
import numpy as np
from jax import lax
from jax.experimental import pallas as pl
from jax.experimental.pallas import tpu as pltpu
from jax.sharding import PartitionSpec as P

CH = 128
BINS = 48
FIRST_BIN = 8
MESH = pl.DeviceIdType.MESH


def spectra_rows(samples, wins):
    bins_here = BINS // wins
    depth = -(-2 * bins_here // 8) * 8
    times = np.arange(samples, dtype=np.int32)[None, :]
    freqs = FIRST_BIN + np.arange(BINS, dtype=np.int32)[:, None]
    phase = (times * freqs % samples).astype(np.float32) * np.float32(2.0 * math.pi / samples)
    both = np.stack([np.cos(phase), -np.sin(phase)], 1).astype(ml_dtypes.bfloat16)
    rows = np.zeros((wins, depth, samples), ml_dtypes.bfloat16)
    rows[:, : 2 * bins_here] = both.reshape(wins, 2 * bins_here, samples)
    return rows.reshape(wins * depth, samples)


def exchange(blks, wins, depth, x_ref, table_ref, white, held, send_sem, recv_sem, loaded):
    blk = lax.axis_index("blk")
    win = lax.axis_index("win")
    sides = ((-1, blk > 0), (1, blk < blks - 1))

    barrier = pltpu.get_barrier_semaphore()

    def greet(step, first):
        for j in range(first, wins):
            pl.semaphore_signal(
                barrier,
                inc=1,
                device_id=(blk + step, lax.rem(win + j, wins)),
                device_id_type=MESH,
            )

    for step, there in sides:
        pl.when(there)(functools.partial(greet, step, 0))
    greet(0, 1)

    loaded()
    spec = lax.dot_general(
        table_ref[...], x_ref[...], (((1,), (1,)), ((), ())), preferred_element_type=jnp.float32
    )
    energy = jnp.sum(spec * spec, axis=0, keepdims=True) * (1.0 / (2 * BINS))
    whitened = spec * lax.rsqrt(energy + 1e-06)
    for v in range(wins):
        part = whitened[v * depth : (v + 1) * depth]
        white[v] = jnp.concatenate(
            [part[:, b * CH : (b + 1) * CH] for b in range(part.shape[1] // CH)], 0
        ).astype(jnp.bfloat16)

    partners = (wins - 1) + wins * ((blk > 0).astype(jnp.int32) + (blk < blks - 1).astype(jnp.int32))
    pl.semaphore_wait(barrier, partners)

    def target(step, j):
        if step == 0 or wins % 2:
            return lax.rem(win + j, wins)
        half = wins // 2
        return 2 * lax.rem(win // 2 + 1 + j % half, half) + j // half

    def copy(step, j):
        v = target(step, j)
        return pltpu.make_async_remote_copy(
            src_ref=white.at[v],
            dst_ref=held.at[1 - step, win],
            send_sem=send_sem.at[1 + step, j],
            recv_sem=recv_sem.at[1 - step, win],
            device_id=(blk + step, v),
            device_id_type=MESH,
        )

    def arrival(step, j):
        v = target(step, j)
        return pltpu.make_async_remote_copy(
            src_ref=white.at[v],
            dst_ref=held.at[1 + step, v],
            send_sem=send_sem.at[1 + step, j],
            recv_sem=recv_sem.at[1 + step, v],
            device_id=(blk + step, v),
            device_id_type=MESH,
        )

    def each(make, act):
        def side(step, first):
            for j in range(first, wins):
                getattr(make(step, j), act)()

        for step, there in sides:
            pl.when(there)(functools.partial(side, step, 0))
        side(0, 1)

    each(copy, "start")
    held[1, win] = white[win]
    each(arrival, "wait_recv")
    return lambda: each(copy, "wait_send")


def operands(wins, depth, pairs_ref, held, left_ref, right_ref):
    blk = lax.axis_index("blk")
    blocks_here = held.shape[2] // depth
    first, second = pairs_ref[0, 0], pairs_ref[0, 1]
    live = first >= 0

    def block(index):
        place = jnp.where(live, index - (blk - 1) * blocks_here, blocks_here)
        place = jnp.clip(place, 0, 3 * blocks_here - 1)
        rows = held[place // blocks_here].astype(jnp.float32)
        which = place % blocks_here
        chosen = rows[:, :depth]
        for b in range(1, blocks_here):
            chosen = jnp.where(which == b, rows[:, b * depth : (b + 1) * depth], chosen)
        return chosen.reshape(wins * depth, CH)

    count = wins * depth
    left_ref[...] = block(first).T.astype(jnp.bfloat16)
    b = block(second) * jnp.where(live, 1.0 / math.sqrt(wins), 0.0).astype(jnp.float32)
    odd = lax.broadcasted_iota(jnp.int32, (count, CH), 0) % 2
    turned = jnp.where(odd == 1, pltpu.roll(b, 1, 0), -pltpu.roll(b, count - 1, 0))
    right_ref[...] = jnp.concatenate([b, turned], 1).astype(jnp.bfloat16)


def spectra_kernel(
    blks, wins, depth, pairs_ref, x_ref, table_ref, left_ref, right_ref,
    x, table, pairs, white, held, send_sem, recv_sem, load_sem,
):
    loads = [
        pltpu.make_async_copy(src, dst, load_sem.at[i])
        for i, (src, dst) in enumerate(((x_ref, x), (table_ref, table), (pairs_ref, pairs)))
    ]
    for load in loads:
        load.start()

    def loaded():
        for load in loads:
            load.wait()

    finish = exchange(blks, wins, depth, x, table, white, held, send_sem, recv_sem, loaded)
    operands(wins, depth, pairs, held, left_ref, right_ref)
    finish()


def cross_kernel(depth, left_ref, right_ref, out_ref, result, sem):
    bins_here = result.shape[1]
    left, right = left_ref[...], right_ref[...]
    bin_of = (lax.broadcasted_iota(jnp.int32, left.shape, 1) % depth) // 2
    writes = []
    for k in range(bins_here):
        both = jnp.dot(
            jnp.where(bin_of == k, left, jnp.zeros_like(left)), right, preferred_element_type=jnp.float32
        )
        for c in range(2):
            result[c, k] = both[:, c * CH : (c + 1) * CH]
            write = pltpu.make_async_copy(result.at[c, k], out_ref.at[c, k], sem.at[c, k])
            write.start()
            writes.append(write)
    for write in writes:
        write.wait()


def solution(mesh):
    blks, wins = mesh.shape["blk"], mesh.shape["win"]

    def shards(traces, pairs):
        rows, windows, samples = traces.shape
        assert windows == 1 and pairs.shape[0] == 1
        table = spectra_rows(samples, wins)
        count = table.shape[0]
        depth = count // wins
        packed = rows // CH * depth
        bins_here = BINS // wins
        inputs = pairs, traces.reshape(rows, samples), jnp.asarray(table)
        left, right = pl.pallas_call(
            functools.partial(spectra_kernel, blks, wins, depth),
            out_shape=[
                pltpu.VMEM((CH, count), jnp.bfloat16),
                pltpu.VMEM((count, 2 * CH), jnp.bfloat16),
            ],
            in_specs=[pl.BlockSpec(memory_space=pltpu.HBM)] * 3,
            out_specs=[pl.BlockSpec(memory_space=pltpu.VMEM)] * 2,
            scratch_shapes=[
                pltpu.VMEM((rows, samples), jnp.bfloat16),
                pltpu.VMEM((count, samples), jnp.bfloat16),
                pltpu.SMEM((1, 2), jnp.int32),
                pltpu.VMEM((wins, packed, CH), jnp.bfloat16),
                pltpu.VMEM((3, wins, packed, CH), jnp.bfloat16),
                pltpu.SemaphoreType.DMA((3, wins)),
                pltpu.SemaphoreType.DMA((3, wins)),
                pltpu.SemaphoreType.DMA((3,)),
            ],
            compiler_params=pltpu.CompilerParams(
                collective_id=0, has_side_effects=True, vmem_limit_bytes=24 << 20
            ),
        )(*(pltpu.with_memory_space_constraint(a, pltpu.HBM) for a in inputs))
        out = pl.pallas_call(
            functools.partial(cross_kernel, depth),
            out_shape=jax.ShapeDtypeStruct((2, bins_here, CH, CH), jnp.float32),
            in_specs=[pl.BlockSpec(memory_space=pltpu.VMEM)] * 2,
            out_specs=pl.BlockSpec(memory_space=pltpu.HBM),
            scratch_shapes=[
                pltpu.VMEM((2, bins_here, CH, CH), jnp.float32),
                pltpu.SemaphoreType.DMA((2, bins_here)),
            ],
            compiler_params=pltpu.CompilerParams(vmem_limit_bytes=24 << 20),
        )(left, right)
        return out[None]

    return jax.shard_map(
        shards,
        mesh=mesh,
        in_specs=(P("blk", "win", None), P("blk", None)),
        out_specs=P("blk", None, "win", None, None),
        check_vma=False,
    )
```

```python
import functools
import math

import jax
import jax.numpy as jnp
import ml_dtypes
import numpy as np
from jax import lax
from jax.experimental import pallas as pl
from jax.experimental.pallas import tpu as pltpu
from jax.sharding import PartitionSpec as P

CH = 128
BINS = 48
FIRST_BIN = 8
MESH = pl.DeviceIdType.MESH


def spectra_rows(samples, wins):
    bins_here = BINS // wins
    depth = -(-2 * bins_here // 8) * 8
    times = np.arange(samples, dtype=np.int32)[None, :]
    freqs = FIRST_BIN + np.arange(BINS, dtype=np.int32)[:, None]
    phase = (times * freqs % samples).astype(np.float32) * np.float32(2.0 * math.pi / samples)
    both = np.stack([np.cos(phase), -np.sin(phase)], 1).astype(ml_dtypes.bfloat16)
    rows = np.zeros((wins, depth, samples), ml_dtypes.bfloat16)
    rows[:, : 2 * bins_here] = both.reshape(wins, 2 * bins_here, samples)
    return rows.reshape(wins * depth, samples)


def exchange(blks, wins, depth, x_ref, table_ref, white, held, send_sem, recv_sem, loaded):
    blk = lax.axis_index("blk")
    win = lax.axis_index("win")
    sides = ((-1, blk > 0), (1, blk < blks - 1))

    barrier = pltpu.get_barrier_semaphore()

    def target(step, j):
        if step == 0 or wins % 2:
            return lax.rem(win + j, wins)
        half = wins // 2
        return 2 * lax.rem(win // 2 + 1 + j % half, half) + j // half

    def greet(step, first):
        for j in range(first, wins):
            pl.semaphore_signal(
                barrier,
                inc=1,
                device_id=(blk + step, target(step, j)),
                device_id_type=MESH,
            )

    for step, there in sides:
        pl.when(there)(functools.partial(greet, step, 0))
    greet(0, 1)

    loaded()
    spec = lax.dot_general(
        table_ref[...], x_ref[...], (((1,), (1,)), ((), ())), preferred_element_type=jnp.float32
    )
    energy = jnp.sum(spec * spec, axis=0, keepdims=True) * (1.0 / (2 * BINS))
    whitened = spec * lax.rsqrt(energy + 1e-06)
    for v in range(wins):
        part = whitened[v * depth : (v + 1) * depth]
        white[v] = jnp.concatenate(
            [part[:, b * CH : (b + 1) * CH] for b in range(part.shape[1] // CH)], 0
        ).astype(jnp.bfloat16)

    partners = (wins - 1) + wins * ((blk > 0).astype(jnp.int32) + (blk < blks - 1).astype(jnp.int32))
    pl.semaphore_wait(barrier, partners)

    def copy(step, j):
        v = target(step, j)
        return pltpu.make_async_remote_copy(
            src_ref=white.at[v],
            dst_ref=held.at[1 - step, win],
            send_sem=send_sem.at[1 + step, j],
            recv_sem=recv_sem.at[1 - step, win],
            device_id=(blk + step, v),
            device_id_type=MESH,
        )

    def arrival(step, j):
        v = target(step, j)
        return pltpu.make_async_remote_copy(
            src_ref=white.at[v],
            dst_ref=held.at[1 + step, v],
            send_sem=send_sem.at[1 + step, j],
            recv_sem=recv_sem.at[1 + step, v],
            device_id=(blk + step, v),
            device_id_type=MESH,
        )

    def each(make, act):
        def side(step, js):
            for j in js:
                getattr(make(step, j), act)()

        for js in (range(wins // 2), range(wins // 2, wins)):
            for step, there in sides:
                pl.when(there)(functools.partial(side, step, js))
        side(0, range(1, wins))

    each(copy, "start")
    held[1, win] = white[win]
    each(arrival, "wait_recv")
    return lambda: each(copy, "wait_send")


def operands(wins, depth, pairs_ref, held, left_ref, right_ref):
    blk = lax.axis_index("blk")
    blocks_here = held.shape[2] // depth
    first, second = pairs_ref[0, 0], pairs_ref[0, 1]
    live = first >= 0

    def block(index):
        place = jnp.where(live, index - (blk - 1) * blocks_here, blocks_here)
        place = jnp.clip(place, 0, 3 * blocks_here - 1)
        rows = held[place // blocks_here].astype(jnp.float32)
        which = place % blocks_here
        chosen = rows[:, :depth]
        for b in range(1, blocks_here):
            chosen = jnp.where(which == b, rows[:, b * depth : (b + 1) * depth], chosen)
        return chosen.reshape(wins * depth, CH)

    count = wins * depth
    left_ref[...] = block(first).T.astype(jnp.bfloat16)
    b = block(second) * jnp.where(live, 1.0 / math.sqrt(wins), 0.0).astype(jnp.float32)
    odd = lax.broadcasted_iota(jnp.int32, (count, CH), 0) % 2
    turned = jnp.where(odd == 1, pltpu.roll(b, 1, 0), -pltpu.roll(b, count - 1, 0))
    right_ref[...] = jnp.concatenate([b, turned], 1).astype(jnp.bfloat16)


def spectra_kernel(
    blks, wins, depth, pairs_ref, x_ref, table_ref, left_ref, right_ref,
    x, table, pairs, white, held, send_sem, recv_sem, load_sem,
):
    loads = [
        pltpu.make_async_copy(src, dst, load_sem.at[i])
        for i, (src, dst) in enumerate(((x_ref, x), (table_ref, table), (pairs_ref, pairs)))
    ]
    for load in loads:
        load.start()

    def loaded():
        for load in loads:
            load.wait()

    finish = exchange(blks, wins, depth, x, table, white, held, send_sem, recv_sem, loaded)
    operands(wins, depth, pairs, held, left_ref, right_ref)
    finish()


def cross_kernel(depth, left_ref, right_ref, out_ref, result, sem):
    bins_here = result.shape[1]
    left, right = left_ref[...], right_ref[...]
    bin_of = (lax.broadcasted_iota(jnp.int32, left.shape, 1) % depth) // 2
    writes = []
    for k in range(bins_here):
        both = jnp.dot(
            jnp.where(bin_of == k, left, jnp.zeros_like(left)), right, preferred_element_type=jnp.float32
        )
        for c in range(2):
            result[c, k] = both[:, c * CH : (c + 1) * CH]
            write = pltpu.make_async_copy(result.at[c, k], out_ref.at[c, k], sem.at[c, k])
            write.start()
            writes.append(write)
    for write in writes:
        write.wait()


def solution(mesh):
    blks, wins = mesh.shape["blk"], mesh.shape["win"]

    def shards(traces, pairs):
        rows, windows, samples = traces.shape
        assert windows == 1 and pairs.shape[0] == 1
        table = spectra_rows(samples, wins)
        count = table.shape[0]
        depth = count // wins
        packed = rows // CH * depth
        bins_here = BINS // wins
        inputs = pairs, traces.reshape(rows, samples), jnp.asarray(table)
        left, right = pl.pallas_call(
            functools.partial(spectra_kernel, blks, wins, depth),
            out_shape=[
                pltpu.VMEM((CH, count), jnp.bfloat16),
                pltpu.VMEM((count, 2 * CH), jnp.bfloat16),
            ],
            in_specs=[pl.BlockSpec(memory_space=pltpu.HBM)] * 3,
            out_specs=[pl.BlockSpec(memory_space=pltpu.VMEM)] * 2,
            scratch_shapes=[
                pltpu.VMEM((rows, samples), jnp.bfloat16),
                pltpu.VMEM((count, samples), jnp.bfloat16),
                pltpu.SMEM((1, 2), jnp.int32),
                pltpu.VMEM((wins, packed, CH), jnp.bfloat16),
                pltpu.VMEM((3, wins, packed, CH), jnp.bfloat16),
                pltpu.SemaphoreType.DMA((3, wins)),
                pltpu.SemaphoreType.DMA((3, wins)),
                pltpu.SemaphoreType.DMA((3,)),
            ],
            compiler_params=pltpu.CompilerParams(
                collective_id=0, has_side_effects=True, vmem_limit_bytes=24 << 20
            ),
        )(*(pltpu.with_memory_space_constraint(a, pltpu.HBM) for a in inputs))
        out = pl.pallas_call(
            functools.partial(cross_kernel, depth),
            out_shape=jax.ShapeDtypeStruct((2, bins_here, CH, CH), jnp.float32),
            in_specs=[pl.BlockSpec(memory_space=pltpu.VMEM)] * 2,
            out_specs=pl.BlockSpec(memory_space=pltpu.HBM),
            scratch_shapes=[
                pltpu.VMEM((2, bins_here, CH, CH), jnp.float32),
                pltpu.SemaphoreType.DMA((2, bins_here)),
            ],
            compiler_params=pltpu.CompilerParams(vmem_limit_bytes=24 << 20),
        )(left, right)
        return out[None]

    return jax.shard_map(
        shards,
        mesh=mesh,
        in_specs=(P("blk", "win", None), P("blk", None)),
        out_specs=P("blk", None, "win", None, None),
        check_vma=False,
    )
```
